32 devices in a mesh: groups: 2 (over y), prow: 8 (over z, x), pcol: 2 (over core).
Axes of the slice: x: 2, y: 2, z: 4, core: 2. Of those that a mesh axis runs over, the one named last changes fastest.
Arguments:
- sigma_root: float32 [12800, 6400], P(('groups', 'prow'), 'pcol'), parts along dimension 0, may hold values from -0.2 to 2.2, as said below
- lower_one: bfloat16 [4, 6400, 512], P(('groups', 'pcol'), 'prow'), parts along dimension 0, may hold values from -0.109375 to 0.109375
- weights_one: float32 [4, 512, 512], P(('groups', 'pcol')), parts along dimension 0, may hold values from -0.2 to 1.4, as said below
- pattern_one: int32 [4, 25, 2], P(('groups', 'pcol')), parts along dimension 0, may hold values 0 or 1
- lower_root: bfloat16 [8, 6400, 256], P(('groups', 'pcol'), 'prow'), parts along dimension 0, may hold values from -0.109375 to 0.109375
- lower_sep: bfloat16 [8, 512, 256], P(('groups', 'pcol'), 'prow'), parts along dimension 0, may hold values from -0.109375 to 0.109375
- weights_two: float32 [8, 256, 256], P(('groups', 'pcol')), parts along dimension 0, may hold values from -0.2 to 1.4, as said below
- pattern_two: int32 [8, 27, 1], P(('groups', 'pcol')), parts along dimension 0, may hold values 0 or 1
Outputs:
- sigma_one_root: float32 [4, 6400, 512], P(('groups', 'pcol'), 'prow'), parts along dimension 0
- sigma_one_diag: float32 [4, 512, 512], P(('groups', 'pcol'), 'prow'), parts along dimension 0
- sigma_two_root: float32 [8, 6400, 256], P(('groups', 'pcol'), 'prow'), parts along dimension 0
- sigma_two_sep: float32 [8, 512, 256], P(('groups', 'pcol'), 'prow'), parts along dimension 0
- sigma_two_diag: float32 [8, 256, 256], P(('groups', 'pcol'), 'prow'), parts along dimension 0
The draws below stay inside these ranges and needn't reach their ends.
There are 2 independent parts, one for each index of `groups`. The reference program is written for one: setup_inputs(seed, part) draws one part's arguments, and reference() takes and returns one part's arrays. A program takes and returns all parts, laid end to end along the dimension named above; each array names one. Nothing has to cross between parts.
Inputs may be any that keep to these rules, and one draw needn't show every extreme that they name: `sigma_root`: symmetric. `weights_one`: lower triangular with diagonal entries of 0.6 to 1.4. `weights_two`: lower triangular with diagonal entries of 0.6 to 1.4.
All inputs are finite; a program needn't handle non-finite values. No bound on the sum of `pattern_one` or of `pattern_two` on one device may be relied on, other than what follows from the above.
Results may differ from the reference program's by a relative error of at most 0.0033.
Values may be sent and summed in bfloat16 or wider, within the bound.
A program may use at most 128 MiB of HBM per device.

```python
import math
import jax
import jax.numpy as jnp
from jax import lax

B = 256
K0 = 25
K1 = 2
K2 = 1
S0 = 6400
S1 = 512
S2 = 256


def lower_triangle(noise, diagonal, scale):
    order_count = noise.shape[-1]
    row_ids = jnp.arange(order_count)[:, None]
    col_ids = jnp.arange(order_count)[None, :]
    below = (row_ids > col_ids).astype(jnp.float32)
    on_diagonal = (row_ids == col_ids).astype(jnp.float32)
    return noise * scale * below + diagonal[..., None] * on_diagonal


def draw_weights_one(key, part):
    key = jax.random.fold_in(key, 21)
    noise_key, diag_key = jax.random.split(key)
    noise = jnp.clip(jax.random.normal(noise_key, (2, S1, S1), jnp.float32), -4.0, 4.0)
    diagonal = jax.random.uniform(diag_key, (2, S1), jnp.float32, 0.6, 1.4)
    return lower_triangle(noise, diagonal, 0.4 / math.sqrt(S1))


def draw_weights_two(key, part):
    key = jax.random.fold_in(key, 22)
    noise_key, diag_key = jax.random.split(key)
    noise = jnp.clip(jax.random.normal(noise_key, (4, S2, S2), jnp.float32), -4.0, 4.0)
    diagonal = jax.random.uniform(diag_key, (4, S2), jnp.float32, 0.6, 1.4)
    return lower_triangle(noise, diagonal, 0.4 / math.sqrt(S2))


def draw_sigma_root(key, part):
    key = jax.random.fold_in(key, 23)
    noise_key, diag_key = jax.random.split(key)
    noise = jnp.clip(jax.random.normal(noise_key, (S0, S0), jnp.float32), -4.0, 4.0)
    symmetric = (noise + noise.T) * (0.35 / math.sqrt(S0))
    diagonal = jnp.exp(jax.random.uniform(diag_key, (S0,), jnp.float32, math.log(0.5), math.log(2.0)))
    on_diagonal = (jnp.arange(S0)[:, None] == jnp.arange(S0)[None, :]).astype(jnp.float32)
    return symmetric + diagonal[:, None] * on_diagonal


def plant(drawn, key, least, high):
    longest = drawn.shape.index(max(drawn.shape))
    spots = []
    for shift in (0, 1):
        where = [jax.random.randint(jax.random.fold_in(key, axis), (), 0, length) for axis, length in enumerate(drawn.shape)]
        where[longest] = (where[longest] + shift) % drawn.shape[longest]
        spots.append(tuple(where))
    return drawn.at[spots[0]].set(least).at[spots[1]].set(high)


def strengthened(array, own_key, source, target, parts, factor):
    def block_of(position):
        return (jnp.arange(array.shape[position]) // (array.shape[position] // parts)).reshape((-1,) + (1,) * (array.ndim - 1 - position))

    near = jax.random.permutation(own_key, parts)[block_of(target)]
    second = (block_of(target) + parts // 2) % parts
    return jnp.where((block_of(source) == near) | (block_of(source) == second), factor * array, array)


def levels(rng, dims, cuts, smallest, largest):
    def one(position, shards_of):
        steps = jax.random.uniform(jax.random.fold_in(jax.random.fold_in(rng, 6), position), (shards_of,), jnp.float32, smallest / len(cuts), largest / len(cuts))
        return jnp.repeat(jnp.exp(steps), dims[position] // shards_of).reshape((-1,) + (1,) * (len(dims) - position - 1))

    loudness = one(*cuts[0])
    for cut in cuts[1:]:
        loudness = loudness * one(*cut)
    return loudness


def noise_with(stream_key, shape, deviation, bound, cuts, heavy, dtype=jnp.bfloat16):
    entries = deviation * jax.random.normal(stream_key, shape, jnp.float32)
    if cuts:
        entries = entries * levels(stream_key, shape, cuts, -0.22, 0.18)
    return jnp.clip(strengthened(entries, jax.random.fold_in(stream_key, 3), *heavy), -bound, bound).astype(dtype)


def setup_inputs(seed: int = 0, part: int = 0) -> dict:
    arg_keys = jax.random.split(jax.random.key(seed), 9)
    own_keys = jax.random.split(jax.random.fold_in(arg_keys[8], part), 9)
    return {
        "sigma_root": draw_sigma_root(jax.random.fold_in(jax.random.fold_in(arg_keys[8], part), 71), part),
        "lower_one": noise_with(own_keys[1], (2, S0, S1), S0 ** -0.5, 0.109375, ((0, 2), (1, 8)), (1, 2, 8, 2.0)),
        "weights_one": draw_weights_one(jax.random.fold_in(jax.random.fold_in(arg_keys[8], part), 71), part),
        "pattern_one": plant((jax.random.randint(own_keys[3], (2, K0, K1), 0, 4) < 3).astype(jnp.int32), jax.random.fold_in(own_keys[3], 1), 0, 1),
        "lower_root": noise_with(own_keys[4], (4, S0, S2), (S0 + S1) ** -0.5, 0.109375, ((0, 2), (1, 8)), (1, 2, 8, 2.0)),
        "lower_sep": noise_with(own_keys[5], (4, S1, S2), (S0 + S1) ** -0.5, 0.109375, ((0, 2), (1, 8)), (1, 2, 8, 2.0)),
        "weights_two": draw_weights_two(jax.random.fold_in(jax.random.fold_in(arg_keys[8], part), 71), part),
        "pattern_two": plant((jax.random.randint(own_keys[7], (4, K0 + K1, K2), 0, 4) < 3).astype(jnp.int32), jax.random.fold_in(own_keys[7], 1), 0, 1),
    }


def expand_pattern(pattern):
    spread = jnp.repeat(pattern.astype(jnp.float32), B, axis=1)
    return jnp.repeat(spread, B, axis=2)


def normalize_factor(lower_part, pattern, weights):
    masked = lower_part.astype(jnp.float32) * expand_pattern(pattern)
    product = jnp.einsum("nrk,nkc->nrc", masked, weights, precision=lax.Precision.HIGHEST)
    return product.astype(jnp.bfloat16)


def reference(sigma_root, lower_one, weights_one, pattern_one, lower_root, lower_sep, weights_two, pattern_two):
    highest = lax.Precision.HIGHEST
    normal_one = normalize_factor(lower_one, pattern_one, weights_one).astype(jnp.float32)
    normal_root = normalize_factor(lower_root, pattern_two[:, :K0, :], weights_two).astype(jnp.float32)
    normal_sep = normalize_factor(lower_sep, pattern_two[:, K0:, :], weights_two).astype(jnp.float32)
    sigma_one_root = -jnp.einsum("rk,nkc->nrc", sigma_root, normal_one, precision=highest)
    sigma_one_diag = jnp.einsum("nkr,nkc->nrc", weights_one, weights_one, precision=highest) - jnp.einsum("nkr,nkc->nrc", normal_one, sigma_one_root, precision=highest)
    parent_root = jnp.repeat(sigma_one_root, 2, axis=0)
    parent_diag = jnp.repeat(sigma_one_diag, 2, axis=0)
    sigma_two_root = -(jnp.einsum("rk,nkc->nrc", sigma_root, normal_root, precision=highest) + jnp.einsum("nrk,nkc->nrc", parent_root, normal_sep, precision=highest))
    sigma_two_sep = -(jnp.einsum("nkr,nkc->nrc", parent_root, normal_root, precision=highest) + jnp.einsum("nrk,nkc->nrc", parent_diag, normal_sep, precision=highest))
    sigma_two_diag = jnp.einsum("nkr,nkc->nrc", weights_two, weights_two, precision=highest) - jnp.einsum("nkr,nkc->nrc", normal_root, sigma_two_root, precision=highest) - jnp.einsum("nkr,nkc->nrc", normal_sep, sigma_two_sep, precision=highest)
    return (sigma_one_root, sigma_one_diag, sigma_two_root, sigma_two_sep, sigma_two_diag)
```

```python
import jax
import jax.numpy as jnp
from jax import lax
from jax.sharding import PartitionSpec as P

B = 256


HIGHEST = lax.Precision.HIGHEST


def expand_pattern(pattern, first_row, row_count, block_width):
    block_ids = (first_row + lax.iota(jnp.int32, row_count)) // block_width
    selector = (block_ids[:, None] == lax.iota(jnp.int32, pattern.shape[1])[None, :]).astype(
        jnp.float32
    )
    spread = jnp.einsum("rk,nkc->nrc", selector, pattern.astype(jnp.float32))
    return jnp.repeat(spread, block_width, axis=2)


def normalize_rows(lower_part, pattern, weights, first_row, block_width):
    masked = lower_part.astype(jnp.float32) * expand_pattern(
        pattern, first_row, lower_part.shape[1], block_width
    )
    return jnp.einsum("nrk,nkc->nrc", masked, weights, precision=HIGHEST).astype(jnp.bfloat16)


def on_device(
    sigma_root, lower_one, weights_one, pattern_one, lower_root, lower_sep, weights_two, pattern_two
):
    grid_rows = lax.axis_size("prow")
    row_index = lax.axis_index("prow")
    root_rows = lower_one.shape[1]
    sep_rows = lower_sep.shape[1]
    sep_two_width = weights_two.shape[2]
    leaf_rows = sep_two_width // grid_rows
    root_blocks = pattern_one.shape[1]
    root_first = row_index * root_rows
    sep_first = row_index * sep_rows
    normal_one = normalize_rows(lower_one, pattern_one, weights_one, root_first, B)
    normal_root = normalize_rows(
        lower_root, pattern_two[:, :root_blocks, :], weights_two, root_first, B
    )
    normal_sep = normalize_rows(
        lower_sep, pattern_two[:, root_blocks:, :], weights_two, sep_first, B
    )
    root_full = lax.all_gather(sigma_root, "pcol", axis=1, tiled=True)
    columns = root_full
    sigma_one_root = -jnp.einsum(
        "rk,nkc->nrc",
        columns,
        lax.all_gather(normal_one, "prow", axis=1, tiled=True).astype(jnp.float32),
        precision=HIGHEST,
    )
    parent_cols = lax.all_to_all(sigma_one_root, "prow", split_axis=2, concat_axis=1, tiled=True)
    piece_float = lax.all_gather(normal_root, "prow", axis=1, tiled=True).astype(jnp.float32)
    columns = root_full
    across = parent_cols[0]
    root_next = jnp.einsum("rk,nkc->nrc", columns, piece_float, precision=HIGHEST)
    sep_next = jnp.einsum("kr,nkc->nrc", across, piece_float, precision=HIGHEST)
    weight_rows = lax.dynamic_slice_in_dim(weights_one, sep_first, sep_rows, 1)
    weight_cols = weight_rows
    normal_cols = normal_one.astype(jnp.float32)
    gram = jnp.einsum("nkr,nkc->rnc", weight_cols, weight_rows, precision=HIGHEST)
    sigma_one_diag = jnp.transpose(
        lax.psum_scatter(
            gram - jnp.einsum("nkr,nkc->rnc", normal_cols, sigma_one_root, precision=HIGHEST),
            "prow",
            scatter_dimension=0,
            tiled=True,
        ),
        (1, 0, 2),
    )
    sep_full = lax.all_gather(normal_sep, "prow", axis=1, tiled=True).astype(jnp.float32)
    sigma_two_root = -(
        root_next + jnp.einsum("rk,nkc->nrc", sigma_one_root[0], sep_full, precision=HIGHEST)
    )
    sigma_two_sep = -(
        sep_next + jnp.einsum("rk,nkc->nrc", sigma_one_diag[0], sep_full, precision=HIGHEST)
    )
    leaf_weights = lax.dynamic_slice_in_dim(weights_two, row_index * leaf_rows, leaf_rows, 1)
    weight_cols = leaf_weights
    root_cols = normal_root.astype(jnp.float32)
    sep_cols = normal_sep.astype(jnp.float32)
    gram = jnp.einsum("nkr,nkc->rnc", weight_cols, leaf_weights, precision=HIGHEST)
    gram = gram - jnp.einsum("nkr,nkc->rnc", root_cols, sigma_two_root, precision=HIGHEST)
    sigma_two_diag = jnp.transpose(
        lax.psum_scatter(
            gram - jnp.einsum("nkr,nkc->rnc", sep_cols, sigma_two_sep, precision=HIGHEST),
            "prow",
            scatter_dimension=0,
            tiled=True,
        ),
        (1, 0, 2),
    )
    return (sigma_one_root, sigma_one_diag, sigma_two_root, sigma_two_sep, sigma_two_diag)


def split_high_low(values):
    high = lax.reduce_precision(values, 8, 7)
    return high.astype(jnp.bfloat16), (values - high).astype(jnp.bfloat16)


def masked_product(lower_part, pattern, weights, first_row):
    mask = expand_pattern(pattern, first_row, lower_part.shape[1], B).astype(jnp.bfloat16)
    masked = lower_part * mask
    high, low = split_high_low(weights)
    both = jnp.einsum(
        "nrk,nkc->nrc", masked, high, preferred_element_type=jnp.float32
    ) + jnp.einsum("nrk,nkc->nrc", masked, low, preferred_element_type=jnp.float32)
    return both.astype(jnp.bfloat16)


def dot(left, right):
    return jnp.dot(left, right, preferred_element_type=jnp.float32)


def dot_rows(left, right):
    return lax.dot_general(
        left, right, (((0,), (0,)), ((), ())), preferred_element_type=jnp.float32
    )


def line_gather(block, layers, layer):
    up, down = [], []
    held_up = held_down = block
    for step in range(1, layers):
        held_up = lax.ppermute(
            held_up,
            "prow",
            [(2 * s + x, 2 * s + 2 + x) for s in range(step - 1, layers - 1) for x in (0, 1)],
        )
        held_down = lax.ppermute(
            held_down,
            "prow",
            [(2 * s + x, 2 * s - 2 + x) for s in range(1, layers - step + 1) for x in (0, 1)],
        )
        up.append(held_up)
        down.append(held_down)
    gathered = jnp.zeros((layers,) + block.shape, block.dtype)
    gathered = lax.dynamic_update_slice(gathered, block[None], (layer, 0, 0))
    for back in range(1, layers):
        piece = jnp.where(layer >= back, up[back - 1], down[layers - back - 1])
        at = lax.rem(layer - back + layers, layers)
        gathered = lax.dynamic_update_slice(gathered, piece[None], (at, 0, 0))
    return gathered


def scatter_sum(parts):
    moved = lax.all_to_all(parts.astype(jnp.bfloat16), "prow", 0, 0, tiled=True)
    return jnp.sum(moved.astype(jnp.float32), axis=0)


def on_pairs(
    sigma_root, lower_one, weights_one, pattern_one, lower_root, lower_sep, weights_two, pattern_two
):
    devices = lax.axis_size("prow")
    layers = devices // 2
    row_index = lax.axis_index("prow")
    core = lax.axis_index("pcol")
    layer, side = row_index // 2, lax.rem(row_index, 2)
    rows = lower_one.shape[1]
    sep_rows = lower_sep.shape[1]
    sep_width = weights_one.shape[2]
    leaf_width = weights_two.shape[2]
    leaf_rows = leaf_width // devices
    root_blocks = pattern_one.shape[1]
    swap_side = [(s, s ^ 1) for s in range(devices)]
    swap_core = [(0, 1), (1, 0)]

    own_one = masked_product(lower_one, pattern_one, weights_one, row_index * rows)[0]
    normal_root = masked_product(
        lower_root, pattern_two[:, :root_blocks, :], weights_two, row_index * rows
    )
    own_two = jnp.concatenate([normal_root[0], normal_root[1]], axis=1)
    normal_sep = masked_product(
        lower_sep, pattern_two[:, root_blocks:, :], weights_two, row_index * sep_rows
    )
    own_sep = jnp.concatenate([normal_sep[0], normal_sep[1]], axis=1)

    half = layers // 2
    by_side = sigma_root.astype(jnp.bfloat16).reshape(rows, half, 2, rows)
    even = by_side[:, :, 0, :].reshape(rows, half * rows)
    odd = by_side[:, :, 1, :].reshape(rows, half * rows)
    kept = jnp.where(side == 0, even, odd)
    given = jnp.where(side == 0, odd, even)
    taken = lax.ppermute(given, "prow", swap_side)
    kept_sibling = lax.ppermute(kept, "pcol", swap_core)
    taken_sibling = lax.ppermute(taken, "pcol", swap_core)

    all_one = line_gather(own_one, layers, layer)
    all_two = line_gather(own_two, layers, layer)
    all_sep = lax.all_gather(own_sep, "prow", axis=0, tiled=True)

    def root_product(gathered):
        width = gathered.shape[2]
        near = lax.dynamic_slice_in_dim(gathered, core * half, half, 0).reshape(-1, width)
        far = lax.dynamic_slice_in_dim(gathered, (1 - core) * half, half, 0).reshape(-1, width)
        away = dot(taken, near) + dot(taken_sibling, far)
        arrived = lax.ppermute(away.astype(jnp.bfloat16), "prow", swap_side)
        return dot(kept, near) + dot(kept_sibling, far) + arrived.astype(jnp.float32)

    product_one = root_product(all_one)
    short_one = product_one.astype(jnp.bfloat16)
    gram_one = dot_rows(own_one, short_one).reshape(devices, sep_rows, sep_width)
    sum_one = scatter_sum(gram_one)
    weight_cols = lax.dynamic_slice_in_dim(weights_one[0], row_index * sep_rows, sep_rows, 1)
    diag_rows = (
        lax.dot_general(
            weight_cols, weights_one[0], (((0,), (0,)), ((), ())), precision=HIGHEST
        )
        + sum_one
    )

    cross = dot_rows(short_one, own_two).reshape(devices, sep_rows, 2 * leaf_width)
    product_two = root_product(all_two)
    two_root = dot(short_one, all_sep) - product_two
    short_two = two_root.astype(jnp.bfloat16)
    leaf_gram = [
        dot_rows(normal_root[b], short_two[:, b * leaf_width : (b + 1) * leaf_width]).reshape(
            devices, leaf_rows, leaf_width
        )
        for b in range(2)
    ]
    sums = scatter_sum(cross)
    sep_two = sums - dot(diag_rows.astype(jnp.bfloat16), all_sep)
    short_sep = sep_two.astype(jnp.bfloat16)
    leaf_gram = [
        leaf_gram[b]
        + dot_rows(normal_sep[b], short_sep[:, b * leaf_width : (b + 1) * leaf_width]).reshape(
            devices, leaf_rows, leaf_width
        )
        for b in range(2)
    ]
    leaf_sum = scatter_sum(jnp.concatenate(leaf_gram, axis=2))
    leaf_cols = lax.dynamic_slice_in_dim(weights_two, row_index * leaf_rows, leaf_rows, 2)
    leaf_square = jnp.einsum("nkr,nkc->nrc", leaf_cols, weights_two, precision=HIGHEST)

    def by_leaf(joined):
        return jnp.stack([joined[:, :leaf_width], joined[:, leaf_width:]])

    return (
        -product_one[None],
        diag_rows[None],
        by_leaf(two_root),
        by_leaf(sep_two),
        leaf_square - by_leaf(leaf_sum),
    )


def solution(mesh):
    placed = (
        P(("groups", "prow"), "pcol"),
        P(("groups", "pcol"), "prow", None),
        P(("groups", "pcol"), None, None),
        P(("groups", "pcol"), None, None),
        P(("groups", "pcol"), "prow", None),
        P(("groups", "pcol"), "prow", None),
        P(("groups", "pcol"), None, None),
        P(("groups", "pcol"), None, None),
    )
    body = on_pairs if mesh.shape["prow"] == 8 else on_device
    return jax.shard_map(
        body,
        mesh=mesh,
        in_specs=placed,
        out_specs=(
            P(("groups", "pcol"), "prow", None),
            P(("groups", "pcol"), "prow", None),
            P(("groups", "pcol"), "prow", None),
            P(("groups", "pcol"), "prow", None),
            P(("groups", "pcol"), "prow", None),
        ),
        check_vma=False,
    )
```

```python
import jax
import jax.numpy as jnp
from jax import lax
from jax.experimental import pallas as pl
from jax.experimental.pallas import tpu as pltpu
from jax.sharding import PartitionSpec as P

B = 256


HIGHEST = lax.Precision.HIGHEST


def expand_pattern(pattern, first_row, row_count, block_width):
    block_ids = (first_row + lax.iota(jnp.int32, row_count)) // block_width
    selector = (block_ids[:, None] == lax.iota(jnp.int32, pattern.shape[1])[None, :]).astype(
        jnp.float32
    )
    spread = jnp.einsum("rk,nkc->nrc", selector, pattern.astype(jnp.float32))
    return jnp.repeat(spread, block_width, axis=2)


def normalize_rows(lower_part, pattern, weights, first_row, block_width):
    masked = lower_part.astype(jnp.float32) * expand_pattern(
        pattern, first_row, lower_part.shape[1], block_width
    )
    return jnp.einsum("nrk,nkc->nrc", masked, weights, precision=HIGHEST).astype(jnp.bfloat16)


def on_device(
    sigma_root, lower_one, weights_one, pattern_one, lower_root, lower_sep, weights_two, pattern_two
):
    grid_rows = lax.axis_size("prow")
    row_index = lax.axis_index("prow")
    root_rows = lower_one.shape[1]
    sep_rows = lower_sep.shape[1]
    sep_two_width = weights_two.shape[2]
    leaf_rows = sep_two_width // grid_rows
    root_blocks = pattern_one.shape[1]
    root_first = row_index * root_rows
    sep_first = row_index * sep_rows
    normal_one = normalize_rows(lower_one, pattern_one, weights_one, root_first, B)
    normal_root = normalize_rows(
        lower_root, pattern_two[:, :root_blocks, :], weights_two, root_first, B
    )
    normal_sep = normalize_rows(
        lower_sep, pattern_two[:, root_blocks:, :], weights_two, sep_first, B
    )
    root_full = lax.all_gather(sigma_root, "pcol", axis=1, tiled=True)
    columns = root_full
    sigma_one_root = -jnp.einsum(
        "rk,nkc->nrc",
        columns,
        lax.all_gather(normal_one, "prow", axis=1, tiled=True).astype(jnp.float32),
        precision=HIGHEST,
    )
    parent_cols = lax.all_to_all(sigma_one_root, "prow", split_axis=2, concat_axis=1, tiled=True)
    piece_float = lax.all_gather(normal_root, "prow", axis=1, tiled=True).astype(jnp.float32)
    columns = root_full
    across = parent_cols[0]
    root_next = jnp.einsum("rk,nkc->nrc", columns, piece_float, precision=HIGHEST)
    sep_next = jnp.einsum("kr,nkc->nrc", across, piece_float, precision=HIGHEST)
    weight_rows = lax.dynamic_slice_in_dim(weights_one, sep_first, sep_rows, 1)
    weight_cols = weight_rows
    normal_cols = normal_one.astype(jnp.float32)
    gram = jnp.einsum("nkr,nkc->rnc", weight_cols, weight_rows, precision=HIGHEST)
    sigma_one_diag = jnp.transpose(
        lax.psum_scatter(
            gram - jnp.einsum("nkr,nkc->rnc", normal_cols, sigma_one_root, precision=HIGHEST),
            "prow",
            scatter_dimension=0,
            tiled=True,
        ),
        (1, 0, 2),
    )
    sep_full = lax.all_gather(normal_sep, "prow", axis=1, tiled=True).astype(jnp.float32)
    sigma_two_root = -(
        root_next + jnp.einsum("rk,nkc->nrc", sigma_one_root[0], sep_full, precision=HIGHEST)
    )
    sigma_two_sep = -(
        sep_next + jnp.einsum("rk,nkc->nrc", sigma_one_diag[0], sep_full, precision=HIGHEST)
    )
    leaf_weights = lax.dynamic_slice_in_dim(weights_two, row_index * leaf_rows, leaf_rows, 1)
    weight_cols = leaf_weights
    root_cols = normal_root.astype(jnp.float32)
    sep_cols = normal_sep.astype(jnp.float32)
    gram = jnp.einsum("nkr,nkc->rnc", weight_cols, leaf_weights, precision=HIGHEST)
    gram = gram - jnp.einsum("nkr,nkc->rnc", root_cols, sigma_two_root, precision=HIGHEST)
    sigma_two_diag = jnp.transpose(
        lax.psum_scatter(
            gram - jnp.einsum("nkr,nkc->rnc", sep_cols, sigma_two_sep, precision=HIGHEST),
            "prow",
            scatter_dimension=0,
            tiled=True,
        ),
        (1, 0, 2),
    )
    return (sigma_one_root, sigma_one_diag, sigma_two_root, sigma_two_sep, sigma_two_diag)


def split_high_low(values):
    high = lax.reduce_precision(values, 8, 7)
    return high.astype(jnp.bfloat16), (values - high).astype(jnp.bfloat16)


def masked_product(lower_part, pattern, weights, first_row):
    mask = expand_pattern(pattern, first_row, lower_part.shape[1], B).astype(jnp.bfloat16)
    masked = lower_part * mask
    high, low = split_high_low(weights)
    both = jnp.einsum(
        "nrk,nkc->nrc", masked, high, preferred_element_type=jnp.float32
    ) + jnp.einsum("nrk,nkc->nrc", masked, low, preferred_element_type=jnp.float32)
    return both.astype(jnp.bfloat16)


def dot(left, right):
    return jnp.dot(left, right, preferred_element_type=jnp.float32)


def dot_rows(left, right):
    return lax.dot_general(
        left, right, (((0,), (0,)), ((), ())), preferred_element_type=jnp.float32
    )


def part_columns(sigma, side):
    rows, columns = sigma.shape
    step = 160 if rows % 160 == 0 else rows
    count = columns // rows

    def kernel(side_ref, sigma_ref, kept_ref, given_ref):
        def pick(first):
            pieces = [
                sigma_ref[:, block * rows : (block + 1) * rows] for block in range(first, count, 2)
            ]
            return jnp.concatenate(pieces, axis=1).astype(jnp.bfloat16)

        @pl.when(side_ref[0] == 0)
        def _():
            kept_ref[...] = pick(0)
            given_ref[...] = pick(1)

        @pl.when(side_ref[0] != 0)
        def _():
            kept_ref[...] = pick(1)
            given_ref[...] = pick(0)

    half = jax.ShapeDtypeStruct((rows, columns // 2), jnp.bfloat16)
    return pl.pallas_call(
        kernel,
        grid=(rows // step,),
        in_specs=[
            pl.BlockSpec(memory_space=pltpu.SMEM),
            pl.BlockSpec((step, columns), lambda i: (i, 0)),
        ],
        out_specs=[pl.BlockSpec((step, columns // 2), lambda i: (i, 0))] * 2,
        out_shape=[half, half],
        compiler_params=pltpu.CompilerParams(vmem_limit_bytes=24 * 2**20),
        cost_estimate=pl.CostEstimate(
            flops=0, bytes_accessed=rows * columns * 6, transcendentals=0
        ),
    )(side.reshape(1), sigma)


def line_gather(block, layers, layer, after=None):
    up, down = [], []
    if after is not None:
        block, _ = lax.optimization_barrier((block, after))
    held_up = held_down = block
    for step in range(1, layers):
        held_up = lax.ppermute(
            held_up,
            "prow",
            [(2 * s + x, 2 * s + 2 + x) for s in range(step - 1, layers - 1) for x in (0, 1)],
        )
        held_down = lax.ppermute(
            held_down,
            "prow",
            [(2 * s + x, 2 * s - 2 + x) for s in range(1, layers - step + 1) for x in (0, 1)],
        )
        up.append(held_up)
        down.append(held_down)
    gathered = jnp.zeros((layers,) + block.shape, block.dtype)
    gathered = lax.dynamic_update_slice(gathered, block[None], (layer, 0, 0))
    for back in range(1, layers):
        piece = jnp.where(layer >= back, up[back - 1], down[layers - back - 1])
        at = lax.rem(layer - back + layers, layers)
        gathered = lax.dynamic_update_slice(gathered, piece[None], (at, 0, 0))
    return gathered, (up[1], down[1])


def scatter_sum(parts):
    moved = lax.all_to_all(parts.astype(jnp.bfloat16), "prow", 0, 0, tiled=True)
    return jnp.sum(moved.astype(jnp.float32), axis=0)


def on_pairs(
    sigma_root, lower_one, weights_one, pattern_one, lower_root, lower_sep, weights_two, pattern_two
):
    devices = lax.axis_size("prow")
    layers = devices // 2
    row_index = lax.axis_index("prow")
    core = lax.axis_index("pcol")
    layer, side = row_index // 2, lax.rem(row_index, 2)
    rows = lower_one.shape[1]
    sep_rows = lower_sep.shape[1]
    sep_width = weights_one.shape[2]
    leaf_width = weights_two.shape[2]
    leaf_rows = leaf_width // devices
    root_blocks = pattern_one.shape[1]
    swap_side = [(s, s ^ 1) for s in range(devices)]
    swap_core = [(0, 1), (1, 0)]

    own_one = masked_product(lower_one, pattern_one, weights_one, row_index * rows)[0]
    normal_root = masked_product(
        lower_root, pattern_two[:, :root_blocks, :], weights_two, row_index * rows
    )
    own_two = jnp.concatenate([normal_root[0], normal_root[1]], axis=1)
    normal_sep = masked_product(
        lower_sep, pattern_two[:, root_blocks:, :], weights_two, row_index * sep_rows
    )
    own_sep = jnp.concatenate([normal_sep[0], normal_sep[1]], axis=1)

    half = layers // 2
    kept, given = part_columns(sigma_root, side)
    taken = lax.ppermute(given, "prow", swap_side)
    kept_sibling = lax.ppermute(kept, "pcol", swap_core)
    taken_sibling = lax.ppermute(taken, "pcol", swap_core)

    joined, late = line_gather(jnp.concatenate([own_one, own_sep]), layers, layer)
    all_one = joined[:, :rows]
    all_two, _ = line_gather(own_two, layers, layer, late)
    sep_here = joined[:, rows:]
    sep_there = lax.ppermute(sep_here, "prow", swap_side)
    all_sep = jnp.where(
        side == 0,
        jnp.stack([sep_here, sep_there], axis=1),
        jnp.stack([sep_there, sep_here], axis=1),
    ).reshape(sep_width, 2 * leaf_width)

    def root_product(gathered):
        width = gathered.shape[2]
        near = lax.dynamic_slice_in_dim(gathered, core * half, half, 0).reshape(-1, width)
        far = lax.dynamic_slice_in_dim(gathered, (1 - core) * half, half, 0).reshape(-1, width)
        away = dot(taken, near) + dot(taken_sibling, far)
        arrived = lax.ppermute(away.astype(jnp.bfloat16), "prow", swap_side)
        return dot(kept, near) + dot(kept_sibling, far) + arrived.astype(jnp.float32)

    product_one = root_product(all_one)
    short_one = product_one.astype(jnp.bfloat16)
    gram_one = dot_rows(own_one, short_one).reshape(devices, sep_rows, sep_width)
    sum_one = scatter_sum(gram_one)
    weight_cols = lax.dynamic_slice_in_dim(weights_one[0], row_index * sep_rows, sep_rows, 1)
    diag_rows = (
        lax.dot_general(
            weight_cols, weights_one[0], (((0,), (0,)), ((), ())), precision=HIGHEST
        )
        + sum_one
    )

    cross = dot_rows(short_one, own_two).reshape(devices, sep_rows, 2 * leaf_width)
    product_two = root_product(all_two)
    two_root = dot(short_one, all_sep) - product_two
    short_two = two_root.astype(jnp.bfloat16)
    leaf_gram = [
        dot_rows(normal_root[b], short_two[:, b * leaf_width : (b + 1) * leaf_width]).reshape(
            devices, leaf_rows, leaf_width
        )
        for b in range(2)
    ]
    sums = scatter_sum(cross)
    sep_two = sums - dot(diag_rows.astype(jnp.bfloat16), all_sep)
    short_sep = sep_two.astype(jnp.bfloat16)
    leaf_gram = [
        leaf_gram[b]
        + dot_rows(normal_sep[b], short_sep[:, b * leaf_width : (b + 1) * leaf_width]).reshape(
            devices, leaf_rows, leaf_width
        )
        for b in range(2)
    ]
    leaf_sum = scatter_sum(jnp.concatenate(leaf_gram, axis=2))
    leaf_cols = lax.dynamic_slice_in_dim(weights_two, row_index * leaf_rows, leaf_rows, 2)
    leaf_square = jnp.einsum("nkr,nkc->nrc", leaf_cols, weights_two, precision=HIGHEST)

    def by_leaf(joined):
        return jnp.stack([joined[:, :leaf_width], joined[:, leaf_width:]])

    return (
        -product_one[None],
        diag_rows[None],
        by_leaf(two_root),
        by_leaf(sep_two),
        leaf_square - by_leaf(leaf_sum),
    )


def solution(mesh):
    placed = (
        P(("groups", "prow"), "pcol"),
        P(("groups", "pcol"), "prow", None),
        P(("groups", "pcol"), None, None),
        P(("groups", "pcol"), None, None),
        P(("groups", "pcol"), "prow", None),
        P(("groups", "pcol"), "prow", None),
        P(("groups", "pcol"), None, None),
        P(("groups", "pcol"), None, None),
    )
    body = on_pairs if mesh.shape["prow"] == 8 else on_device
    return jax.shard_map(
        body,
        mesh=mesh,
        in_specs=placed,
        out_specs=(
            P(("groups", "pcol"), "prow", None),
            P(("groups", "pcol"), "prow", None),
            P(("groups", "pcol"), "prow", None),
            P(("groups", "pcol"), "prow", None),
            P(("groups", "pcol"), "prow", None),
        ),
        check_vma=False,
    )
```

```python
import jax
import jax.numpy as jnp
from jax import lax
from jax.experimental import pallas as pl
from jax.experimental.pallas import tpu as pltpu
from jax.sharding import PartitionSpec as P

B = 256


HIGHEST = lax.Precision.HIGHEST


def expand_pattern(pattern, first_row, row_count, block_width):
    block_ids = (first_row + lax.iota(jnp.int32, row_count)) // block_width
    selector = (block_ids[:, None] == lax.iota(jnp.int32, pattern.shape[1])[None, :]).astype(
        jnp.float32
    )
    spread = jnp.einsum("rk,nkc->nrc", selector, pattern.astype(jnp.float32))
    return jnp.repeat(spread, block_width, axis=2)


def normalize_rows(lower_part, pattern, weights, first_row, block_width):
    masked = lower_part.astype(jnp.float32) * expand_pattern(
        pattern, first_row, lower_part.shape[1], block_width
    )
    return jnp.einsum("nrk,nkc->nrc", masked, weights, precision=HIGHEST).astype(jnp.bfloat16)


def on_device(
    sigma_root, lower_one, weights_one, pattern_one, lower_root, lower_sep, weights_two, pattern_two
):
    grid_rows = lax.axis_size("prow")
    row_index = lax.axis_index("prow")
    root_rows = lower_one.shape[1]
    sep_rows = lower_sep.shape[1]
    sep_two_width = weights_two.shape[2]
    leaf_rows = sep_two_width // grid_rows
    root_blocks = pattern_one.shape[1]
    root_first = row_index * root_rows
    sep_first = row_index * sep_rows
    normal_one = normalize_rows(lower_one, pattern_one, weights_one, root_first, B)
    normal_root = normalize_rows(
        lower_root, pattern_two[:, :root_blocks, :], weights_two, root_first, B
    )
    normal_sep = normalize_rows(
        lower_sep, pattern_two[:, root_blocks:, :], weights_two, sep_first, B
    )
    root_full = lax.all_gather(sigma_root, "pcol", axis=1, tiled=True)
    columns = root_full
    sigma_one_root = -jnp.einsum(
        "rk,nkc->nrc",
        columns,
        lax.all_gather(normal_one, "prow", axis=1, tiled=True).astype(jnp.float32),
        precision=HIGHEST,
    )
    parent_cols = lax.all_to_all(sigma_one_root, "prow", split_axis=2, concat_axis=1, tiled=True)
    piece_float = lax.all_gather(normal_root, "prow", axis=1, tiled=True).astype(jnp.float32)
    columns = root_full
    across = parent_cols[0]
    root_next = jnp.einsum("rk,nkc->nrc", columns, piece_float, precision=HIGHEST)
    sep_next = jnp.einsum("kr,nkc->nrc", across, piece_float, precision=HIGHEST)
    weight_rows = lax.dynamic_slice_in_dim(weights_one, sep_first, sep_rows, 1)
    weight_cols = weight_rows
    normal_cols = normal_one.astype(jnp.float32)
    gram = jnp.einsum("nkr,nkc->rnc", weight_cols, weight_rows, precision=HIGHEST)
    sigma_one_diag = jnp.transpose(
        lax.psum_scatter(
            gram - jnp.einsum("nkr,nkc->rnc", normal_cols, sigma_one_root, precision=HIGHEST),
            "prow",
            scatter_dimension=0,
            tiled=True,
        ),
        (1, 0, 2),
    )
    sep_full = lax.all_gather(normal_sep, "prow", axis=1, tiled=True).astype(jnp.float32)
    sigma_two_root = -(
        root_next + jnp.einsum("rk,nkc->nrc", sigma_one_root[0], sep_full, precision=HIGHEST)
    )
    sigma_two_sep = -(
        sep_next + jnp.einsum("rk,nkc->nrc", sigma_one_diag[0], sep_full, precision=HIGHEST)
    )
    leaf_weights = lax.dynamic_slice_in_dim(weights_two, row_index * leaf_rows, leaf_rows, 1)
    weight_cols = leaf_weights
    root_cols = normal_root.astype(jnp.float32)
    sep_cols = normal_sep.astype(jnp.float32)
    gram = jnp.einsum("nkr,nkc->rnc", weight_cols, leaf_weights, precision=HIGHEST)
    gram = gram - jnp.einsum("nkr,nkc->rnc", root_cols, sigma_two_root, precision=HIGHEST)
    sigma_two_diag = jnp.transpose(
        lax.psum_scatter(
            gram - jnp.einsum("nkr,nkc->rnc", sep_cols, sigma_two_sep, precision=HIGHEST),
            "prow",
            scatter_dimension=0,
            tiled=True,
        ),
        (1, 0, 2),
    )
    return (sigma_one_root, sigma_one_diag, sigma_two_root, sigma_two_sep, sigma_two_diag)


def split_high_low(values):
    high = lax.reduce_precision(values, 8, 7)
    return high.astype(jnp.bfloat16), (values - high).astype(jnp.bfloat16)


def masked_product(lower_part, pattern, weights, first_row):
    mask = expand_pattern(pattern, first_row, lower_part.shape[1], B).astype(jnp.bfloat16)
    masked = lower_part * mask
    high, low = split_high_low(weights)
    both = jnp.einsum(
        "nrk,nkc->nrc", masked, high, preferred_element_type=jnp.float32
    ) + jnp.einsum("nrk,nkc->nrc", masked, low, preferred_element_type=jnp.float32)
    return both.astype(jnp.bfloat16)


def dot(left, right):
    return jnp.dot(left, right, preferred_element_type=jnp.float32)


def dot_rows(left, right):
    return lax.dot_general(
        left, right, (((0,), (0,)), ((), ())), preferred_element_type=jnp.float32
    )


def part_columns(sigma, side):
    rows, columns = sigma.shape
    step = 160 if rows % 160 == 0 else rows
    count = columns // rows

    def kernel(side_ref, sigma_ref, kept_ref, given_ref):
        def pick(first):
            pieces = [
                sigma_ref[:, block * rows : (block + 1) * rows] for block in range(first, count, 2)
            ]
            return jnp.concatenate(pieces, axis=1).astype(jnp.bfloat16)

        @pl.when(side_ref[0] == 0)
        def _():
            kept_ref[...] = pick(0)
            given_ref[...] = pick(1)

        @pl.when(side_ref[0] != 0)
        def _():
            kept_ref[...] = pick(1)
            given_ref[...] = pick(0)

    half = jax.ShapeDtypeStruct((rows, columns // 2), jnp.bfloat16)
    return pl.pallas_call(
        kernel,
        grid=(rows // step,),
        in_specs=[
            pl.BlockSpec(memory_space=pltpu.SMEM),
            pl.BlockSpec((step, columns), lambda i: (i, 0)),
        ],
        out_specs=[pl.BlockSpec((step, columns // 2), lambda i: (i, 0))] * 2,
        out_shape=[half, half],
        compiler_params=pltpu.CompilerParams(vmem_limit_bytes=24 * 2**20),
        cost_estimate=pl.CostEstimate(
            flops=0, bytes_accessed=rows * columns * 6, transcendentals=0
        ),
    )(side.reshape(1), sigma)


def line_hop(held, layers, step):
    up = [(2 * s + x, 2 * s + 2 + x) for s in range(step - 1, layers - 1) for x in (0, 1)]
    down = [(2 * s + x, 2 * s - 2 + x) for s in range(1, layers - step + 1) for x in (0, 1)]
    return lax.ppermute(held[0], "prow", up), lax.ppermute(held[1], "prow", down)


def line_order(block, hops, layers, layer):
    gathered = jnp.zeros((layers,) + block.shape, block.dtype)
    gathered = lax.dynamic_update_slice(gathered, block[None], (layer, 0, 0))
    for back in range(1, layers):
        piece = jnp.where(layer >= back, hops[back - 1][0], hops[layers - back - 1][1])
        at = lax.rem(layer - back + layers, layers)
        gathered = lax.dynamic_update_slice(gathered, piece[None], (at, 0, 0))
    return gathered


def tie(values, after):
    return lax.optimization_barrier((values, after))[0]


def scatter_sum(parts):
    moved = lax.all_to_all(parts.astype(jnp.bfloat16), "prow", 0, 0, tiled=True)
    return jnp.sum(moved.astype(jnp.float32), axis=0)


def on_pairs(
    sigma_root, lower_one, weights_one, pattern_one, lower_root, lower_sep, weights_two, pattern_two
):
    devices = lax.axis_size("prow")
    layers = devices // 2
    row_index = lax.axis_index("prow")
    core = lax.axis_index("pcol")
    layer, side = row_index // 2, lax.rem(row_index, 2)
    rows = lower_one.shape[1]
    sep_rows = lower_sep.shape[1]
    sep_width = weights_one.shape[2]
    leaf_width = weights_two.shape[2]
    leaf_rows = leaf_width // devices
    root_blocks = pattern_one.shape[1]
    swap_side = [(s, s ^ 1) for s in range(devices)]
    swap_core = [(0, 1), (1, 0)]

    own_one = masked_product(lower_one, pattern_one, weights_one, row_index * rows)[0]
    normal_root = masked_product(
        lower_root, pattern_two[:, :root_blocks, :], weights_two, row_index * rows
    )
    own_two = jnp.concatenate([normal_root[0], normal_root[1]], axis=1)
    normal_sep = masked_product(
        lower_sep, pattern_two[:, root_blocks:, :], weights_two, row_index * sep_rows
    )
    own_sep = jnp.concatenate([normal_sep[0], normal_sep[1]], axis=1)

    half = layers // 2
    kept, given = part_columns(sigma_root, side)
    taken = lax.ppermute(given, "prow", swap_side)
    kept_sibling = lax.ppermute(kept, "pcol", swap_core)
    taken_sibling = lax.ppermute(taken, "pcol", swap_core)

    def root_parts(gathered):
        width = gathered.shape[2]
        near = lax.dynamic_slice_in_dim(gathered, core * half, half, 0).reshape(-1, width)
        far = lax.dynamic_slice_in_dim(gathered, (1 - core) * half, half, 0).reshape(-1, width)
        away = (dot(taken, near) + dot(taken_sibling, far)).astype(jnp.bfloat16)
        return near, far, away

    def root_total(near, far, arrived):
        return dot(kept, near) + dot(kept_sibling, far) + arrived.astype(jnp.float32)

    first = jnp.concatenate([own_one, own_sep])
    hops_one = [line_hop((first, first), layers, 1)]
    second = tie(own_two, hops_one[0])
    hops_two = []
    held = (second, second)
    for step in range(2, layers):
        hops_one.append(line_hop(hops_one[-1], layers, step))
        held = line_hop(held, layers, step - 1)
        hops_two.append(held)
    joined = line_order(first, hops_one, layers, layer)
    near_one, far_one, away_one = root_parts(joined[:, :rows])
    arrived_one = lax.ppermute(away_one, "prow", swap_side)
    sep_here = joined[:, rows:]
    sep_there = lax.ppermute(sep_here, "prow", swap_side)
    hops_two.append(line_hop(tie(held, away_one), layers, layers - 1))

    product_one = root_total(near_one, far_one, arrived_one)
    short_one = product_one.astype(jnp.bfloat16)
    packed = dot_rows(short_one, jnp.concatenate([own_one, own_two], axis=1)).astype(jnp.bfloat16)
    packed = packed.reshape(devices, sep_rows, -1)
    all_sep = jnp.where(
        side == 0,
        jnp.stack([sep_here, sep_there], axis=1),
        jnp.stack([sep_there, sep_here], axis=1),
    ).reshape(sep_width, 2 * leaf_width)
    hops_two[-1] = tie(hops_two[-1], packed)
    sums = scatter_sum(packed)
    weight_cols = lax.dynamic_slice_in_dim(weights_one[0], row_index * sep_rows, sep_rows, 1)
    diag_rows = (
        lax.dot_general(
            weight_cols, weights_one[0], (((0,), (0,)), ((), ())), precision=HIGHEST
        )
        + sums[:, :sep_width]
    )
    sep_two = sums[:, sep_width:] - dot(diag_rows.astype(jnp.bfloat16), all_sep)
    short_sep = sep_two.astype(jnp.bfloat16)

    near_two, far_two, away_two = root_parts(line_order(own_two, hops_two, layers, layer))
    arrived_two = lax.ppermute(away_two, "prow", swap_side)
    product_two = root_total(near_two, far_two, arrived_two)
    two_root = dot(short_one, all_sep) - product_two
    short_two = two_root.astype(jnp.bfloat16)
    leaf_gram = [
        (
            dot_rows(normal_root[b], short_two[:, b * leaf_width : (b + 1) * leaf_width])
            + dot_rows(normal_sep[b], short_sep[:, b * leaf_width : (b + 1) * leaf_width])
        ).reshape(devices, leaf_rows, leaf_width)
        for b in range(2)
    ]
    leaf_sum = scatter_sum(jnp.concatenate(leaf_gram, axis=2))
    leaf_cols = lax.dynamic_slice_in_dim(weights_two, row_index * leaf_rows, leaf_rows, 2)
    leaf_square = jnp.einsum("nkr,nkc->nrc", leaf_cols, weights_two, precision=HIGHEST)

    def by_leaf(joined):
        return jnp.stack([joined[:, :leaf_width], joined[:, leaf_width:]])

    return (
        -product_one[None],
        diag_rows[None],
        by_leaf(two_root),
        by_leaf(sep_two),
        leaf_square - by_leaf(leaf_sum),
    )


def solution(mesh):
    placed = (
        P(("groups", "prow"), "pcol"),
        P(("groups", "pcol"), "prow", None),
        P(("groups", "pcol"), None, None),
        P(("groups", "pcol"), None, None),
        P(("groups", "pcol"), "prow", None),
        P(("groups", "pcol"), "prow", None),
        P(("groups", "pcol"), None, None),
        P(("groups", "pcol"), None, None),
    )
    body = on_pairs if mesh.shape["prow"] == 8 else on_device
    return jax.shard_map(
        body,
        mesh=mesh,
        in_specs=placed,
        out_specs=(
            P(("groups", "pcol"), "prow", None),
            P(("groups", "pcol"), "prow", None),
            P(("groups", "pcol"), "prow", None),
            P(("groups", "pcol"), "prow", None),
            P(("groups", "pcol"), "prow", None),
        ),
        check_vma=False,
    )
```

```python
import jax
import jax.numpy as jnp
from jax import lax
from jax.experimental import pallas as pl
from jax.experimental.pallas import tpu as pltpu
from jax.sharding import PartitionSpec as P

B = 256


HIGHEST = lax.Precision.HIGHEST


def expand_pattern(pattern, first_row, row_count, block_width):
    block_ids = (first_row + lax.iota(jnp.int32, row_count)) // block_width
    selector = (block_ids[:, None] == lax.iota(jnp.int32, pattern.shape[1])[None, :]).astype(
        jnp.float32
    )
    spread = jnp.einsum("rk,nkc->nrc", selector, pattern.astype(jnp.float32))
    return jnp.repeat(spread, block_width, axis=2)


def normalize_rows(lower_part, pattern, weights, first_row, block_width):
    masked = lower_part.astype(jnp.float32) * expand_pattern(
        pattern, first_row, lower_part.shape[1], block_width
    )
    return jnp.einsum("nrk,nkc->nrc", masked, weights, precision=HIGHEST).astype(jnp.bfloat16)


def on_device(
    sigma_root, lower_one, weights_one, pattern_one, lower_root, lower_sep, weights_two, pattern_two
):
    grid_rows = lax.axis_size("prow")
    row_index = lax.axis_index("prow")
    root_rows = lower_one.shape[1]
    sep_rows = lower_sep.shape[1]
    sep_two_width = weights_two.shape[2]
    leaf_rows = sep_two_width // grid_rows
    root_blocks = pattern_one.shape[1]
    root_first = row_index * root_rows
    sep_first = row_index * sep_rows
    normal_one = normalize_rows(lower_one, pattern_one, weights_one, root_first, B)
    normal_root = normalize_rows(
        lower_root, pattern_two[:, :root_blocks, :], weights_two, root_first, B
    )
    normal_sep = normalize_rows(
        lower_sep, pattern_two[:, root_blocks:, :], weights_two, sep_first, B
    )
    root_full = lax.all_gather(sigma_root, "pcol", axis=1, tiled=True)
    columns = root_full
    sigma_one_root = -jnp.einsum(
        "rk,nkc->nrc",
        columns,
        lax.all_gather(normal_one, "prow", axis=1, tiled=True).astype(jnp.float32),
        precision=HIGHEST,
    )
    parent_cols = lax.all_to_all(sigma_one_root, "prow", split_axis=2, concat_axis=1, tiled=True)
    piece_float = lax.all_gather(normal_root, "prow", axis=1, tiled=True).astype(jnp.float32)
    columns = root_full
    across = parent_cols[0]
    root_next = jnp.einsum("rk,nkc->nrc", columns, piece_float, precision=HIGHEST)
    sep_next = jnp.einsum("kr,nkc->nrc", across, piece_float, precision=HIGHEST)
    weight_rows = lax.dynamic_slice_in_dim(weights_one, sep_first, sep_rows, 1)
    weight_cols = weight_rows
    normal_cols = normal_one.astype(jnp.float32)
    gram = jnp.einsum("nkr,nkc->rnc", weight_cols, weight_rows, precision=HIGHEST)
    sigma_one_diag = jnp.transpose(
        lax.psum_scatter(
            gram - jnp.einsum("nkr,nkc->rnc", normal_cols, sigma_one_root, precision=HIGHEST),
            "prow",
            scatter_dimension=0,
            tiled=True,
        ),
        (1, 0, 2),
    )
    sep_full = lax.all_gather(normal_sep, "prow", axis=1, tiled=True).astype(jnp.float32)
    sigma_two_root = -(
        root_next + jnp.einsum("rk,nkc->nrc", sigma_one_root[0], sep_full, precision=HIGHEST)
    )
    sigma_two_sep = -(
        sep_next + jnp.einsum("rk,nkc->nrc", sigma_one_diag[0], sep_full, precision=HIGHEST)
    )
    leaf_weights = lax.dynamic_slice_in_dim(weights_two, row_index * leaf_rows, leaf_rows, 1)
    weight_cols = leaf_weights
    root_cols = normal_root.astype(jnp.float32)
    sep_cols = normal_sep.astype(jnp.float32)
    gram = jnp.einsum("nkr,nkc->rnc", weight_cols, leaf_weights, precision=HIGHEST)
    gram = gram - jnp.einsum("nkr,nkc->rnc", root_cols, sigma_two_root, precision=HIGHEST)
    sigma_two_diag = jnp.transpose(
        lax.psum_scatter(
            gram - jnp.einsum("nkr,nkc->rnc", sep_cols, sigma_two_sep, precision=HIGHEST),
            "prow",
            scatter_dimension=0,
            tiled=True,
        ),
        (1, 0, 2),
    )
    return (sigma_one_root, sigma_one_diag, sigma_two_root, sigma_two_sep, sigma_two_diag)


def split_high_low(values):
    high = lax.reduce_precision(values, 8, 7)
    return high.astype(jnp.bfloat16), (values - high).astype(jnp.bfloat16)


def masked_product(lower_part, pattern, weights, first_row):
    block_ids = (first_row + lax.iota(jnp.int32, lower_part.shape[1])) // B
    picked = (block_ids[:, None] == lax.iota(jnp.int32, pattern.shape[1])[None, :])[None, :, :, None]
    spread = jnp.sum(jnp.where(picked, pattern[:, None], 0), axis=2).astype(jnp.bfloat16)
    masked = jnp.concatenate(
        [
            lower_part[:, :, k * B : (k + 1) * B] * spread[:, :, k : k + 1]
            for k in range(pattern.shape[2])
        ],
        axis=2,
    )
    high, low = split_high_low(weights)
    both = jnp.einsum(
        "nrk,nkc->nrc", masked, high, preferred_element_type=jnp.float32
    ) + jnp.einsum("nrk,nkc->nrc", masked, low, preferred_element_type=jnp.float32)
    return both.astype(jnp.bfloat16)


def dot(left, right):
    return jnp.dot(left, right, preferred_element_type=jnp.float32)


def dot_rows(left, right):
    return lax.dot_general(
        left, right, (((0,), (0,)), ((), ())), preferred_element_type=jnp.float32
    )


def part_columns(sigma, side):
    rows, columns = sigma.shape
    step = 160 if rows % 160 == 0 else rows
    count = columns // rows

    def kernel(side_ref, sigma_ref, kept_ref, given_ref):
        def pick(first):
            pieces = [
                sigma_ref[:, block * rows : (block + 1) * rows] for block in range(first, count, 2)
            ]
            return jnp.concatenate(pieces, axis=1).astype(jnp.bfloat16)

        @pl.when(side_ref[0] == 0)
        def _():
            kept_ref[...] = pick(0)
            given_ref[...] = pick(1)

        @pl.when(side_ref[0] != 0)
        def _():
            kept_ref[...] = pick(1)
            given_ref[...] = pick(0)

    half = jax.ShapeDtypeStruct((rows, columns // 2), jnp.bfloat16)
    return pl.pallas_call(
        kernel,
        grid=(rows // step,),
        in_specs=[
            pl.BlockSpec(memory_space=pltpu.SMEM),
            pl.BlockSpec((step, columns), lambda i: (i, 0)),
        ],
        out_specs=[pl.BlockSpec((step, columns // 2), lambda i: (i, 0))] * 2,
        out_shape=[half, half],
        compiler_params=pltpu.CompilerParams(vmem_limit_bytes=24 * 2**20),
        cost_estimate=pl.CostEstimate(
            flops=0, bytes_accessed=rows * columns * 6, transcendentals=0
        ),
    )(side.reshape(1), sigma)


def line_hop(held, layers, step):
    up = [(2 * s + x, 2 * s + 2 + x) for s in range(step - 1, layers - 1) for x in (0, 1)]
    down = [(2 * s + x, 2 * s - 2 + x) for s in range(1, layers - step + 1) for x in (0, 1)]
    return lax.ppermute(held[0], "prow", up), lax.ppermute(held[1], "prow", down)


def line_order(block, hops, layers, layer, first):
    by_distance = [block] + [
        jnp.where(layer >= back, hops[back - 1][0], hops[layers - back - 1][1])
        for back in range(1, layers)
    ]

    def at(place):
        back = lax.rem(layer - place + 2 * layers, layers)
        found = by_distance[0]
        for distance in range(1, layers):
            found = jnp.where(back == distance, by_distance[distance], found)
        return found

    return [at(first + place) for place in range(layers)]


def tie(values, after):
    return lax.optimization_barrier((values, after))[0]


def scatter_sum(parts):
    moved = lax.all_to_all(parts.astype(jnp.bfloat16), "prow", 0, 0, tiled=True)
    return jnp.sum(moved.astype(jnp.float32), axis=0)


def on_pairs(
    sigma_root, lower_one, weights_one, pattern_one, lower_root, lower_sep, weights_two, pattern_two
):
    devices = lax.axis_size("prow")
    layers = devices // 2
    row_index = lax.axis_index("prow")
    core = lax.axis_index("pcol")
    layer, side = row_index // 2, lax.rem(row_index, 2)
    rows = lower_one.shape[1]
    sep_rows = lower_sep.shape[1]
    sep_width = weights_one.shape[2]
    leaf_width = weights_two.shape[2]
    leaf_rows = leaf_width // devices
    root_blocks = pattern_one.shape[1]
    swap_side = [(s, s ^ 1) for s in range(devices)]
    swap_core = [(0, 1), (1, 0)]

    own_one = masked_product(lower_one, pattern_one, weights_one, row_index * rows)[0]
    normal_root = masked_product(
        lower_root, pattern_two[:, :root_blocks, :], weights_two, row_index * rows
    )
    own_two = jnp.concatenate([normal_root[0], normal_root[1]], axis=1)
    normal_sep = masked_product(
        lower_sep, pattern_two[:, root_blocks:, :], weights_two, row_index * sep_rows
    )
    own_sep = jnp.concatenate([normal_sep[0], normal_sep[1]], axis=1)

    first = jnp.concatenate([own_one, own_sep])
    half = layers // 2
    kept, given = part_columns(sigma_root, tie(side, first))
    taken = lax.ppermute(given, "prow", swap_side)
    kept_sibling = lax.ppermute(kept, "pcol", swap_core)
    taken_sibling = lax.ppermute(taken, "pcol", swap_core)

    def root_parts(gathered):
        near = jnp.concatenate(gathered[:half])
        far = jnp.concatenate(gathered[half:])
        away = (dot(taken, near) + dot(taken_sibling, far)).astype(jnp.bfloat16)
        return near, far, away

    def root_total(near, far, arrived):
        return dot(kept, near) + dot(kept_sibling, far) + arrived.astype(jnp.float32)

    hops_one = [line_hop((first, first), layers, 1)]
    second = tie(own_two, first)
    hops_two = []
    held = (second, second)
    for step in range(2, layers):
        hops_one.append(line_hop(hops_one[-1], layers, step))
        held = line_hop(held, layers, step - 1)
        hops_two.append(held)
    def order(block, hops):
        return line_order(block, hops, layers, layer, core * half)

    near_one, far_one, away_one = root_parts(
        order(own_one, [[held[:rows] for held in hop] for hop in hops_one])
    )
    arrived_one = lax.ppermute(away_one, "prow", swap_side)
    sep_here = jnp.stack(
        line_order(
            own_sep, [[held[rows:] for held in hop] for hop in hops_one], layers, layer, 0
        )
    )
    sep_there = lax.ppermute(sep_here, "prow", swap_side)
    hops_two.append(line_hop(tie(held, away_one), layers, layers - 1))

    product_one = root_total(near_one, far_one, arrived_one)
    short_one = product_one.astype(jnp.bfloat16)
    packed = dot_rows(short_one, jnp.concatenate([own_one, own_two], axis=1)).astype(jnp.bfloat16)
    packed = packed.reshape(devices, sep_rows, -1)
    all_sep = jnp.where(
        side == 0,
        jnp.stack([sep_here, sep_there], axis=1),
        jnp.stack([sep_there, sep_here], axis=1),
    ).reshape(sep_width, 2 * leaf_width)
    hops_two[-1] = tie(hops_two[-1], packed)
    sums = scatter_sum(packed)
    weight_cols = lax.dynamic_slice_in_dim(weights_one[0], row_index * sep_rows, sep_rows, 1)
    diag_rows = (
        lax.dot_general(
            weight_cols, weights_one[0], (((0,), (0,)), ((), ())), precision=HIGHEST
        )
        + sums[:, :sep_width]
    )
    sep_two = sums[:, sep_width:] - dot(diag_rows.astype(jnp.bfloat16), all_sep)
    short_sep = sep_two.astype(jnp.bfloat16)

    near_two, far_two, away_two = root_parts(order(own_two, hops_two))
    arrived_two = lax.ppermute(away_two, "prow", swap_side)
    product_two = root_total(near_two, far_two, arrived_two)
    two_root = dot(short_one, all_sep) - product_two
    short_two = two_root.astype(jnp.bfloat16)
    leaf_gram = [
        (
            dot_rows(normal_root[b], short_two[:, b * leaf_width : (b + 1) * leaf_width])
            + dot_rows(normal_sep[b], short_sep[:, b * leaf_width : (b + 1) * leaf_width])
        ).reshape(devices, leaf_rows, leaf_width)
        for b in range(2)
    ]
    leaf_sum = scatter_sum(jnp.concatenate(leaf_gram, axis=2))
    leaf_cols = lax.dynamic_slice_in_dim(weights_two, row_index * leaf_rows, leaf_rows, 2)
    leaf_square = jnp.einsum("nkr,nkc->nrc", leaf_cols, weights_two, precision=HIGHEST)

    def by_leaf(joined):
        return jnp.stack([joined[:, :leaf_width], joined[:, leaf_width:]])

    return (
        -product_one[None],
        diag_rows[None],
        by_leaf(two_root),
        by_leaf(sep_two),
        leaf_square - by_leaf(leaf_sum),
    )


def solution(mesh):
    placed = (
        P(("groups", "prow"), "pcol"),
        P(("groups", "pcol"), "prow", None),
        P(("groups", "pcol"), None, None),
        P(("groups", "pcol"), None, None),
        P(("groups", "pcol"), "prow", None),
        P(("groups", "pcol"), "prow", None),
        P(("groups", "pcol"), None, None),
        P(("groups", "pcol"), None, None),
    )
    body = on_pairs if mesh.shape["prow"] == 8 else on_device
    return jax.shard_map(
        body,
        mesh=mesh,
        in_specs=placed,
        out_specs=(
            P(("groups", "pcol"), "prow", None),
            P(("groups", "pcol"), "prow", None),
            P(("groups", "pcol"), "prow", None),
            P(("groups", "pcol"), "prow", None),
            P(("groups", "pcol"), "prow", None),
        ),
        check_vma=False,
    )
```

```python
import jax
import jax.numpy as jnp
from jax import lax
from jax.experimental import pallas as pl
from jax.experimental.pallas import tpu as pltpu
from jax.sharding import PartitionSpec as P

B = 256


HIGHEST = lax.Precision.HIGHEST


def expand_pattern(pattern, first_row, row_count, block_width):
    block_ids = (first_row + lax.iota(jnp.int32, row_count)) // block_width
    selector = (block_ids[:, None] == lax.iota(jnp.int32, pattern.shape[1])[None, :]).astype(
        jnp.float32
    )
    spread = jnp.einsum("rk,nkc->nrc", selector, pattern.astype(jnp.float32))
    return jnp.repeat(spread, block_width, axis=2)


def normalize_rows(lower_part, pattern, weights, first_row, block_width):
    masked = lower_part.astype(jnp.float32) * expand_pattern(
        pattern, first_row, lower_part.shape[1], block_width
    )
    return jnp.einsum("nrk,nkc->nrc", masked, weights, precision=HIGHEST).astype(jnp.bfloat16)


def on_device(
    sigma_root, lower_one, weights_one, pattern_one, lower_root, lower_sep, weights_two, pattern_two
):
    grid_rows = lax.axis_size("prow")
    row_index = lax.axis_index("prow")
    root_rows = lower_one.shape[1]
    sep_rows = lower_sep.shape[1]
    sep_two_width = weights_two.shape[2]
    leaf_rows = sep_two_width // grid_rows
    root_blocks = pattern_one.shape[1]
    root_first = row_index * root_rows
    sep_first = row_index * sep_rows
    normal_one = normalize_rows(lower_one, pattern_one, weights_one, root_first, B)
    normal_root = normalize_rows(
        lower_root, pattern_two[:, :root_blocks, :], weights_two, root_first, B
    )
    normal_sep = normalize_rows(
        lower_sep, pattern_two[:, root_blocks:, :], weights_two, sep_first, B
    )
    root_full = lax.all_gather(sigma_root, "pcol", axis=1, tiled=True)
    columns = root_full
    sigma_one_root = -jnp.einsum(
        "rk,nkc->nrc",
        columns,
        lax.all_gather(normal_one, "prow", axis=1, tiled=True).astype(jnp.float32),
        precision=HIGHEST,
    )
    parent_cols = lax.all_to_all(sigma_one_root, "prow", split_axis=2, concat_axis=1, tiled=True)
    piece_float = lax.all_gather(normal_root, "prow", axis=1, tiled=True).astype(jnp.float32)
    columns = root_full
    across = parent_cols[0]
    root_next = jnp.einsum("rk,nkc->nrc", columns, piece_float, precision=HIGHEST)
    sep_next = jnp.einsum("kr,nkc->nrc", across, piece_float, precision=HIGHEST)
    weight_rows = lax.dynamic_slice_in_dim(weights_one, sep_first, sep_rows, 1)
    weight_cols = weight_rows
    normal_cols = normal_one.astype(jnp.float32)
    gram = jnp.einsum("nkr,nkc->rnc", weight_cols, weight_rows, precision=HIGHEST)
    sigma_one_diag = jnp.transpose(
        lax.psum_scatter(
            gram - jnp.einsum("nkr,nkc->rnc", normal_cols, sigma_one_root, precision=HIGHEST),
            "prow",
            scatter_dimension=0,
            tiled=True,
        ),
        (1, 0, 2),
    )
    sep_full = lax.all_gather(normal_sep, "prow", axis=1, tiled=True).astype(jnp.float32)
    sigma_two_root = -(
        root_next + jnp.einsum("rk,nkc->nrc", sigma_one_root[0], sep_full, precision=HIGHEST)
    )
    sigma_two_sep = -(
        sep_next + jnp.einsum("rk,nkc->nrc", sigma_one_diag[0], sep_full, precision=HIGHEST)
    )
    leaf_weights = lax.dynamic_slice_in_dim(weights_two, row_index * leaf_rows, leaf_rows, 1)
    weight_cols = leaf_weights
    root_cols = normal_root.astype(jnp.float32)
    sep_cols = normal_sep.astype(jnp.float32)
    gram = jnp.einsum("nkr,nkc->rnc", weight_cols, leaf_weights, precision=HIGHEST)
    gram = gram - jnp.einsum("nkr,nkc->rnc", root_cols, sigma_two_root, precision=HIGHEST)
    sigma_two_diag = jnp.transpose(
        lax.psum_scatter(
            gram - jnp.einsum("nkr,nkc->rnc", sep_cols, sigma_two_sep, precision=HIGHEST),
            "prow",
            scatter_dimension=0,
            tiled=True,
        ),
        (1, 0, 2),
    )
    return (sigma_one_root, sigma_one_diag, sigma_two_root, sigma_two_sep, sigma_two_diag)


def split_high_low(values):
    high = lax.reduce_precision(values, 8, 7)
    return high.astype(jnp.bfloat16), (values - high).astype(jnp.bfloat16)


def masked_product(lower_part, pattern, weights, first_row):
    block_ids = (first_row + lax.iota(jnp.int32, lower_part.shape[1])) // B
    picked = (block_ids[:, None] == lax.iota(jnp.int32, pattern.shape[1])[None, :])[None, :, :, None]
    spread = jnp.sum(jnp.where(picked, pattern[:, None], 0), axis=2).astype(jnp.bfloat16)
    masked = jnp.concatenate(
        [
            lower_part[:, :, k * B : (k + 1) * B] * spread[:, :, k : k + 1]
            for k in range(pattern.shape[2])
        ],
        axis=2,
    )
    high, low = split_high_low(weights)
    both = jnp.einsum(
        "nrk,nkc->nrc", masked, high, preferred_element_type=jnp.float32
    ) + jnp.einsum("nrk,nkc->nrc", masked, low, preferred_element_type=jnp.float32)
    return both.astype(jnp.bfloat16)


def dot(left, right):
    return jnp.dot(left, right, preferred_element_type=jnp.float32)


def dot_rows(left, right):
    return lax.dot_general(
        left, right, (((0,), (0,)), ((), ())), preferred_element_type=jnp.float32
    )


def part_columns(sigma, side):
    rows, columns = sigma.shape
    step = 160 if rows % 160 == 0 else rows
    count = columns // rows

    def kernel(side_ref, sigma_ref, kept_ref, given_ref):
        def pick(first):
            pieces = [
                sigma_ref[:, block * rows : (block + 1) * rows] for block in range(first, count, 2)
            ]
            return jnp.concatenate(pieces, axis=1).astype(jnp.bfloat16)

        @pl.when(side_ref[0] == 0)
        def _():
            kept_ref[...] = pick(0)
            given_ref[...] = pick(1)

        @pl.when(side_ref[0] != 0)
        def _():
            kept_ref[...] = pick(1)
            given_ref[...] = pick(0)

    half = jax.ShapeDtypeStruct((rows, columns // 2), jnp.bfloat16)
    return pl.pallas_call(
        kernel,
        grid=(rows // step,),
        in_specs=[
            pl.BlockSpec(memory_space=pltpu.SMEM),
            pl.BlockSpec((step, columns), lambda i: (i, 0)),
        ],
        out_specs=[pl.BlockSpec((step, columns // 2), lambda i: (i, 0))] * 2,
        out_shape=[half, half],
        compiler_params=pltpu.CompilerParams(vmem_limit_bytes=24 * 2**20),
        cost_estimate=pl.CostEstimate(
            flops=0, bytes_accessed=rows * columns * 6, transcendentals=0
        ),
    )(side.reshape(1), sigma)


def line_hop(held, layers, step):
    up = [(2 * s + x, 2 * s + 2 + x) for s in range(step - 1, layers - 1) for x in (0, 1)]
    down = [(2 * s + x, 2 * s - 2 + x) for s in range(1, layers - step + 1) for x in (0, 1)]
    return lax.ppermute(held[0], "prow", up), lax.ppermute(held[1], "prow", down)


def line_order(block, hops, layers, layer):
    gathered = jnp.zeros((layers,) + block.shape, block.dtype)
    gathered = lax.dynamic_update_slice(gathered, block[None], (layer, 0, 0))
    for back in range(1, layers):
        piece = jnp.where(layer >= back, hops[back - 1][0], hops[layers - back - 1][1])
        at = lax.rem(layer - back + layers, layers)
        gathered = lax.dynamic_update_slice(gathered, piece[None], (at, 0, 0))
    return gathered


def line_pick(block, hops, layers, layer, first):
    by_distance = [block] + [
        jnp.where(layer >= back, hops[back - 1][0], hops[layers - back - 1][1])
        for back in range(1, layers)
    ]

    def at(place):
        back = lax.rem(layer - place + 2 * layers, layers)
        found = by_distance[0]
        for distance in range(1, layers):
            found = jnp.where(back == distance, by_distance[distance], found)
        return found

    return [at(first + place) for place in range(layers)]


def tie(values, after):
    return lax.optimization_barrier((values, after))[0]


def scatter_sum(parts):
    moved = lax.all_to_all(parts.astype(jnp.bfloat16), "prow", 0, 0, tiled=True)
    return jnp.sum(moved.astype(jnp.float32), axis=0)


def on_pairs(
    sigma_root, lower_one, weights_one, pattern_one, lower_root, lower_sep, weights_two, pattern_two
):
    devices = lax.axis_size("prow")
    layers = devices // 2
    row_index = lax.axis_index("prow")
    core = lax.axis_index("pcol")
    layer, side = row_index // 2, lax.rem(row_index, 2)
    rows = lower_one.shape[1]
    sep_rows = lower_sep.shape[1]
    sep_width = weights_one.shape[2]
    leaf_width = weights_two.shape[2]
    leaf_rows = leaf_width // devices
    root_blocks = pattern_one.shape[1]
    swap_side = [(s, s ^ 1) for s in range(devices)]
    swap_core = [(0, 1), (1, 0)]

    own_one = masked_product(lower_one, pattern_one, weights_one, row_index * rows)[0]
    normal_root = masked_product(
        lower_root, pattern_two[:, :root_blocks, :], weights_two, row_index * rows
    )
    own_two = jnp.concatenate([normal_root[0], normal_root[1]], axis=1)
    normal_sep = masked_product(
        lower_sep, pattern_two[:, root_blocks:, :], weights_two, row_index * sep_rows
    )
    own_sep = jnp.concatenate([normal_sep[0], normal_sep[1]], axis=1)

    half = layers // 2
    kept, given = part_columns(sigma_root, side)
    taken = lax.ppermute(given, "prow", swap_side)
    kept_sibling = lax.ppermute(kept, "pcol", swap_core)
    taken_sibling = lax.ppermute(taken, "pcol", swap_core)

    def root_parts(gathered):
        width = gathered.shape[2]
        near = lax.dynamic_slice_in_dim(gathered, core * half, half, 0).reshape(-1, width)
        far = lax.dynamic_slice_in_dim(gathered, (1 - core) * half, half, 0).reshape(-1, width)
        away = (dot(taken, near) + dot(taken_sibling, far)).astype(jnp.bfloat16)
        return near, far, away

    def root_total(near, far, arrived):
        return dot(kept, near) + dot(kept_sibling, far) + arrived.astype(jnp.float32)

    first = jnp.concatenate([own_one, own_sep])
    hops_one = [line_hop((first, first), layers, 1)]
    second = tie(own_two, hops_one[0])
    hops_two = []
    held = (second, second)
    for step in range(2, layers):
        hops_one.append(line_hop(hops_one[-1], layers, step))
        held = line_hop(held, layers, step - 1)
        hops_two.append(held)
    joined = line_order(first, hops_one, layers, layer)
    near_one, far_one, away_one = root_parts(joined[:, :rows])
    arrived_one = lax.ppermute(away_one, "prow", swap_side)
    sep_here = joined[:, rows:]
    sep_there = lax.ppermute(sep_here, "prow", swap_side)
    hops_two.append(line_hop(tie(held, away_one), layers, layers - 1))

    product_one = root_total(near_one, far_one, arrived_one)
    short_one = product_one.astype(jnp.bfloat16)
    packed = dot_rows(short_one, jnp.concatenate([own_one, own_two], axis=1)).astype(jnp.bfloat16)
    packed = packed.reshape(devices, sep_rows, -1)
    all_sep = jnp.where(
        side == 0,
        jnp.stack([sep_here, sep_there], axis=1),
        jnp.stack([sep_there, sep_here], axis=1),
    ).reshape(sep_width, 2 * leaf_width)
    hops_two[-1] = tie(hops_two[-1], packed)
    sums = scatter_sum(packed)
    weight_cols = lax.dynamic_slice_in_dim(weights_one[0], row_index * sep_rows, sep_rows, 1)
    diag_rows = (
        lax.dot_general(
            weight_cols, weights_one[0], (((0,), (0,)), ((), ())), precision=HIGHEST
        )
        + sums[:, :sep_width]
    )
    sep_two = sums[:, sep_width:] - dot(diag_rows.astype(jnp.bfloat16), all_sep)
    short_sep = sep_two.astype(jnp.bfloat16)

    picked = line_pick(own_two, hops_two, layers, layer, core * half)
    near_two, far_two = jnp.concatenate(picked[:half]), jnp.concatenate(picked[half:])
    away_two = (dot(taken, near_two) + dot(taken_sibling, far_two)).astype(jnp.bfloat16)
    arrived_two = lax.ppermute(away_two, "prow", swap_side)
    product_two = root_total(near_two, far_two, arrived_two)
    two_root = dot(short_one, all_sep) - product_two
    short_two = two_root.astype(jnp.bfloat16)
    leaf_gram = [
        (
            dot_rows(normal_root[b], short_two[:, b * leaf_width : (b + 1) * leaf_width])
            + dot_rows(normal_sep[b], short_sep[:, b * leaf_width : (b + 1) * leaf_width])
        ).reshape(devices, leaf_rows, leaf_width)
        for b in range(2)
    ]
    leaf_sum = scatter_sum(jnp.concatenate(leaf_gram, axis=2))
    leaf_cols = lax.dynamic_slice_in_dim(weights_two, row_index * leaf_rows, leaf_rows, 2)
    leaf_square = jnp.einsum("nkr,nkc->nrc", leaf_cols, weights_two, precision=HIGHEST)

    def by_leaf(joined):
        return jnp.stack([joined[:, :leaf_width], joined[:, leaf_width:]])

    return (
        -product_one[None],
        diag_rows[None],
        by_leaf(two_root),
        by_leaf(sep_two),
        leaf_square - by_leaf(leaf_sum),
    )


def solution(mesh):
    placed = (
        P(("groups", "prow"), "pcol"),
        P(("groups", "pcol"), "prow", None),
        P(("groups", "pcol"), None, None),
        P(("groups", "pcol"), None, None),
        P(("groups", "pcol"), "prow", None),
        P(("groups", "pcol"), "prow", None),
        P(("groups", "pcol"), None, None),
        P(("groups", "pcol"), None, None),
    )
    body = on_pairs if mesh.shape["prow"] == 8 else on_device
    return jax.shard_map(
        body,
        mesh=mesh,
        in_specs=placed,
        out_specs=(
            P(("groups", "pcol"), "prow", None),
            P(("groups", "pcol"), "prow", None),
            P(("groups", "pcol"), "prow", None),
            P(("groups", "pcol"), "prow", None),
            P(("groups", "pcol"), "prow", None),
        ),
        check_vma=False,
    )
```
